256 devices in a mesh: freq: 8 (over y_hi, x), chan: 32 (over z, y_lo, core).
Axes of the slice: x: 4, y: 4 (y_hi: 2, y_lo: 2; y = y_hi * 2 + y_lo), z: 8, core: 2. Of those that a mesh axis runs over, the one named last changes fastest.
Arguments:
- spectra: bfloat16 [2, 128, 2048, 256], P(None, 'freq', 'chan'), may hold values from -500 to 500
Outputs:
- correlation: float32 [128, 2048, 2048], P(None, 'chan', 'freq')
The draws below stay inside these ranges and needn't reach their ends.
All inputs are finite; a program needn't handle non-finite values.
Results may differ from the reference program's by a relative error of at most 0.0052.
Values may be sent and summed in bfloat16 or wider, within the bound.
No kernel may reach another device: no remote copies, remote signals or barrier semaphores. Data moves between devices by JAX's collectives and lax.ppermute only.
A program may use at most 128 MiB of HBM per device.

```python
import math
import jax
import jax.numpy as jnp
from jax import lax

CH_DEV = 64
W = 256
LAGS = 128
NF = 128
NCH = 2048
N_CHAN = 32


def draw_spectra(key, part):
    key = jax.random.fold_in(key, 11)
    key_base, key_chan, key_window = jax.random.split(key, 3)
    base = jnp.clip(jax.random.normal(key_base, (2, NF, NCH, W), jnp.float32), -5.0, 5.0)
    top = 10.0
    chan_scale = jnp.exp(jax.random.uniform(key_chan, (1, NF, NCH, 1), jnp.float32, 0.0, jnp.log(top)))
    window_scale = jnp.exp(jax.random.uniform(key_window, (1, NF, 1, W), jnp.float32, 0.0, jnp.log(top)))
    return (base * chan_scale * window_scale).astype(jnp.bfloat16)


def setup_inputs(seed: int = 0) -> dict:
    splits = jax.random.split(jax.random.key(seed), 2)
    spectra = draw_spectra(jax.random.fold_in(splits[1], 71), 0)
    return {"spectra": spectra}


def lag_table(count_f, lags):
    freqs = jnp.arange(count_f, dtype=jnp.int32)
    shifts = jnp.arange(lags, dtype=jnp.int32)
    turns = shifts[:, None] * freqs[None, :] % lags
    angle = 2.0 * math.pi / lags * turns.astype(jnp.float32)
    return jnp.stack([jnp.cos(angle), -jnp.sin(angle)], axis=1).astype(jnp.bfloat16)

def reference(spectra):
    values = spectra.astype(jnp.float32)
    power = lax.optimization_barrier(jnp.mean(values[0] * values[0] + values[1] * values[1], axis=-1, keepdims=True))
    white = (values * lax.rsqrt(power + 1e-06)[None]).astype(jnp.bfloat16)
    rows_all = jnp.stack([white, jnp.stack([white[1], -white[0]])])
    rows_all = rows_all.reshape(2, 2, NF, N_CHAN, CH_DEV, W)
    blocks = jnp.moveaxis(rows_all, 3, 0)
    columns = white.astype(jnp.float32)
    table = lag_table(NF, LAGS).astype(jnp.float32)
    factor = jnp.sqrt(jnp.float32(W) / jnp.float32(NF))

    def one_block(rows):
        cross = jnp.einsum('qpfiw,pfjw->qfij', rows.astype(jnp.float32), columns) * (1.0 / W)
        cross = cross.astype(jnp.bfloat16).astype(jnp.float32)
        return jnp.einsum('lpf,pfij->lij', table, cross) * factor
    result = lax.map(one_block, blocks)
    return jnp.transpose(result, (1, 0, 2, 3)).reshape(LAGS, NCH, NCH)
```

```python
import functools
import math

import jax
import jax.numpy as jnp
import ml_dtypes
import numpy as np
from jax import lax
from jax.experimental import pallas as pl
from jax.experimental.pallas import tpu as pltpu
from jax.sharding import Mesh, PartitionSpec as P

LAGS = 128
NF = 128
W = 256
CH = 64
X, YH, Z, YL, CO = 4, 2, 8, 2, 2
NK = YH * X
NQ = YL * CO
PLANE = ("yh", "x", "yl", "co")
VMEM = 56 * 1024 * 1024


def lag_matrix():
    out = np.zeros((LAGS, NK, NQ, 2, 2), np.float32)
    lags = np.arange(LAGS)
    step = np.float32(2.0 * math.pi / LAGS)

    def angle(f):
        return step * (lags * f % LAGS).astype(np.float32)

    for k in range(NK):
        group, side = min(k, 7 - k), int(k > 3)
        for q in range(NQ):
            for t in range(2):
                m = 2 * (side * NQ + q) + t
                if m == 0 and group == 3:
                    out[:, k, q, t, 0] = np.cos(angle(0))
                    out[:, k, q, t, 1] = np.cos(angle(64))
                else:
                    f = 16 * group + m if m else 16 * (group + 1)
                    out[:, k, q, t, 0] = np.cos(angle(f))
                    out[:, k, q, t, 1] = -np.sin(angle(f))
    return out.reshape(LAGS, NK * NQ * 4).astype(ml_dtypes.bfloat16)


def whiten_kernel(hi_ref, x_ref, sp_ref, o_ref, *, t):
    x = x_ref[:, 0].astype(jnp.float32)
    if t == 0:
        take = jnp.logical_and(hi_ref[0] == 0, pl.program_id(0) == 0)
        x = jnp.where(take, sp_ref[...].astype(jnp.float32), x)
    power = jnp.sum(x[0] * x[0] + x[1] * x[1], axis=-1, keepdims=True) * (1.0 / W)
    o_ref[0] = (x * lax.rsqrt(power + 1e-06)[None]).astype(jnp.bfloat16)


def whiten(spectra, special, hi, t):
    def source(r, hi_ref):
        m = 2 * r + t
        return (0, jnp.where(hi_ref[0] == 0, m, lax.rem(16 - m, 16)), 0, 0)

    return pl.pallas_call(
        functools.partial(whiten_kernel, t=t),
        grid_spec=pltpu.PrefetchScalarGridSpec(
            num_scalar_prefetch=1,
            grid=(8,),
            in_specs=[
                pl.BlockSpec((2, 1, CH, W), source),
                pl.BlockSpec((2, CH, W), lambda r, hi_ref: (0, 0, 0)),
            ],
            out_specs=pl.BlockSpec((1, 2, CH, W), lambda r, hi_ref: (r, 0, 0, 0)),
        ),
        out_shape=jax.ShapeDtypeStruct((8, 2, CH, W), jnp.bfloat16),
        compiler_params=pltpu.CompilerParams(vmem_limit_bytes=VMEM),
        cost_estimate=pl.CostEstimate(flops=2000000, bytes_accessed=1 << 20, transcendentals=0),
        name="whiten",
    )(hi, spectra, special)


def cross_kernel(h, has_prev, z_ref, coef_ref, y_ref, *refs):
    if has_prev:
        refs = refs[1:]
    ups, dns, out_ref, left = refs[0:4], refs[4:8], refs[8], refs[9]
    step = pl.program_id(0)

    @pl.when(step == 0)
    def _():
        for side in range(2):
            re = y_ref[side, :, 0].reshape(4 * CH, W).astype(jnp.float32)
            im = y_ref[side, :, 1].reshape(4 * CH, W).astype(jnp.float32)
            for o in range(2):
                alpha = coef_ref[o * 4 + side * 2]
                beta = coef_ref[o * 4 + side * 2 + 1]
                left[o, side, 0] = (alpha * re + beta * im).astype(jnp.bfloat16)
                left[o, side, 1] = (alpha * im - beta * re).astype(jnp.bfloat16)

    def emit(pieces):
        for o in range(2):
            acc = None
            for side in range(2):
                for p in range(2):
                    part = lax.dot_general(
                        left[o, side, p],
                        pieces(side, p),
                        (((1,), (1,)), ((), ())),
                        preferred_element_type=jnp.float32,
                    )
                    acc = part if acc is None else acc + part
            acc = (acc * (1.0 / W)).astype(jnp.bfloat16)
            out_ref[0, :, 0, o] = acc.reshape(4, CH, 128)

    def block(ref):
        return lambda side, p: ref[side, :, p].reshape(2 * CH, W)

    @pl.when(step == 0)
    def _():
        emit(lambda side, p: y_ref[side, 2 * h:2 * h + 2, p].reshape(2 * CH, W))

    for s in range(3):
        @pl.when(step == 2 * s + 1)
        def _(s=s):
            emit(block(ups[s]))

        @pl.when(step == 2 * s + 2)
        def _(s=s):
            emit(block(dns[s]))

    @pl.when(step == 7)
    def _():
        emit(lambda side, p: (ups, dns)[side][3][0, :, p].reshape(2 * CH, W))


def cross(zpos, coef, y, ups, dns, prev, h, slot, slots):

    def whole(shape):
        return pl.BlockSpec(shape, lambda s, *_: (0,) * len(shape))

    def target(s, z_ref, coef_ref):
        dist = lax.div(s + 1, 2)
        g = lax.rem(z_ref[0] + 8 + jnp.where(lax.rem(s, 2) == 1, -dist, dist), 8)
        return (g, 0, slot, 0, 0, 0)

    has_prev = prev is not None
    ins = [y] + ([prev] if has_prev else []) + list(ups) + list(dns)
    specs = [whole(y.shape)]
    if has_prev:
        specs.append(pl.BlockSpec(memory_space=pl.ANY))
    specs += [whole(b.shape) for b in list(ups) + list(dns)]
    return pl.pallas_call(
        functools.partial(cross_kernel, h, has_prev),
        grid_spec=pltpu.PrefetchScalarGridSpec(
            num_scalar_prefetch=2,
            grid=(8,),
            in_specs=specs,
            out_specs=pl.BlockSpec((1, 4, 1, 2, CH, 128), target),
            scratch_shapes=[pltpu.VMEM((2, 2, 2, 4 * CH, W), jnp.bfloat16)],
        ),
        out_shape=jax.ShapeDtypeStruct((8, 4, slots, 2, CH, 128), jnp.bfloat16),
        input_output_aliases={3: 0} if has_prev else {},
        compiler_params=pltpu.CompilerParams(vmem_limit_bytes=VMEM),
        cost_estimate=pl.CostEstimate(flops=1 << 30, bytes_accessed=7 << 19, transcendentals=0),
        name="cross",
    )(zpos, coef, *ins)


def lags_kernel(has_prev, t_ref, x_ref, *refs):
    out_ref, wide = refs[-2:]
    rows = 16
    n = NK * NQ * 4
    wide[...] = x_ref[...].reshape(n, rows, 128).astype(jnp.float32).reshape(n * rows, 128)
    out = out_ref.reshape(LAGS * rows, 128)
    for i in range(rows):
        x = wide[pl.ds(i, n, stride=rows), :].astype(jnp.bfloat16)
        y = jnp.dot(t_ref[...], x, preferred_element_type=jnp.float32)
        out[pl.ds(i, LAGS, stride=rows), :] = y * math.sqrt(W / NF)


def lags(table, moved, prev, h):
    has_prev = prev is not None
    n = NK * NQ * 4
    ins = [table, moved] + ([prev] if has_prev else [])
    specs = [
        pl.BlockSpec((LAGS, n), lambda i: (0, 0)),
        pl.BlockSpec((NK * NQ, 2, 2, 16, 128), lambda i: (0, 0, 0, i, 0)),
    ]
    if has_prev:
        specs.append(pl.BlockSpec(memory_space=pl.ANY))
    return pl.pallas_call(
        functools.partial(lags_kernel, has_prev),
        grid=(CH // 16,),
        in_specs=specs,
        out_specs=pl.BlockSpec((LAGS, 16, 128), lambda i: (0, i, h)),
        out_shape=jax.ShapeDtypeStruct((LAGS, CH, 256), jnp.float32),
        scratch_shapes=[pltpu.VMEM((n * 16, 128), jnp.float32)],
        input_output_aliases={2: 0} if has_prev else {},
        compiler_params=pltpu.CompilerParams(vmem_limit_bytes=VMEM),
        cost_estimate=pl.CostEstimate(flops=1 << 28, bytes_accessed=6 << 20, transcendentals=0),
        name="lags",
    )(*ins)


def shards(spectra):
    k = lax.axis_index("yh") * X + lax.axis_index("x")
    q = lax.axis_index("yl") * CO + lax.axis_index("co")
    hi = (k > 3).astype(jnp.int32)
    zpos = lax.axis_index("z").astype(jnp.int32).reshape(1)

    special = lax.ppermute(spectra[:, 0], ("yh", "x"), [(1, 0), (2, 1), (3, 2), (0, 3)])
    groups = [[j * NQ + i for j in (g, 7 - g) for i in range(NQ)] for g in range(4)]

    def regroup(t):
        sent = whiten(spectra, special, hi.reshape(1), t)
        got = lax.all_to_all(
            sent, PLANE, split_axis=0, concat_axis=0, tiled=True, axis_index_groups=groups
        )
        return got.reshape(2, NQ, 2, CH, W)

    sin0 = -math.sin(0.0)
    sin64 = -math.sin(math.pi)
    regular = np.array([1, 0, 1, 0, 0, 1, 0, -1], np.float32)
    selfs = np.array([1, sin0, 0, 0, 0, 0, 1, sin64], np.float32)
    is_self = jnp.logical_and(k == 3, q == 0)
    coefs = {0: jnp.where(is_self, selfs, regular), 1: jnp.asarray(regular)}

    up = [(i, (i + 1) % Z) for i in range(Z)]
    dn = [((i + 1) % Z, i) for i in range(Z)]

    def ring(chunk):
        a = b = chunk
        ups, dns = [], []
        for _ in range(3):
            a = lax.ppermute(a, "z", up)
            b = lax.ppermute(b, "z", dn)
            ups.append(a)
            dns.append(b)
        ups.append(lax.ppermute(a[0:1], "z", up))
        dns.append(lax.ppermute(b[1:2], "z", dn))
        return ups, dns

    table = jnp.asarray(lag_matrix())
    ys = {1: regroup(1), 0: regroup(0)}
    out = None
    for h in range(2):
        parts = None
        for t in (1, 0):
            ups, dns = ring(ys[t][:, 2 * h:2 * h + 2])
            parts = cross(zpos, coefs[t], ys[t], ups, dns, parts, h, t, 2)
        parts = parts.reshape(NK * NQ, 2, 2, CH, 128)
        moved = lax.all_to_all(parts, PLANE, split_axis=0, concat_axis=0, tiled=True)
        out = lags(table, moved, out, h)
    return out


def solution(mesh):
    fine = Mesh(mesh.devices.reshape(YH, X, Z, YL, CO), ("yh", "x", "z", "yl", "co"))
    return jax.shard_map(
        shards,
        mesh=fine,
        in_specs=(P(None, ("yh", "x"), ("z", "yl", "co"), None),),
        out_specs=P(None, ("z", "yl", "co"), ("yh", "x")),
        check_vma=False,
    )
```

```python
import functools
import math

import jax
import jax.numpy as jnp
import ml_dtypes
import numpy as np
from jax import lax
from jax.experimental import pallas as pl
from jax.experimental.pallas import tpu as pltpu
from jax.sharding import Mesh, PartitionSpec as P

LAGS = 128
NF = 128
W = 256
CH = 64
COLS = 256
X, YH, Z, YL, CO = 4, 2, 8, 2, 2
NK = YH * X
NQ = YL * CO
PLANE = ("yh", "x", "yl", "co")
VMEM = 56 * 1024 * 1024
ROWS = 32
FLOPS = 3 << 32


def lag_matrix():
    out = np.zeros((LAGS, 2, NK, NQ, 2), np.float32)
    lags = np.arange(LAGS)
    step = np.float32(2.0 * math.pi / LAGS)

    def angle(f):
        return step * (lags * f % LAGS).astype(np.float32)

    for k in range(NK):
        group, side = min(k, 7 - k), int(k > 3)
        for q in range(NQ):
            for t in range(2):
                m = 2 * (side * NQ + q) + t
                if m == 0 and group == 3:
                    out[:, t, k, q, 0] = np.cos(angle(0))
                    out[:, t, k, q, 1] = np.cos(angle(64))
                else:
                    f = 16 * group + m if m else 16 * (group + 1)
                    out[:, t, k, q, 0] = np.cos(angle(f))
                    out[:, t, k, q, 1] = -np.sin(angle(f))
    return out[:, ::-1].reshape(LAGS, NK * NQ * 4).astype(ml_dtypes.bfloat16)


def whiten_kernel(t, hi_ref, x_ref, *refs):
    o_ref = refs[-1]
    hi = hi_ref[0] == 1
    for j in range(4):
        u = pl.program_id(0) * 4 + j
        x = x_ref[:, j, 0].astype(jnp.float32)
        if t == 0 and j == 0:
            take = jnp.logical_and(jnp.logical_not(hi), pl.program_id(0) == 0)
            x = jnp.where(take, refs[0][...].astype(jnp.float32), x)
        power = jnp.sum(x[0] * x[0] + x[1] * x[1], axis=-1, keepdims=True) * (1.0 / W)
        r = jnp.where(hi, 7 - u if t else lax.rem(8 - u, 8), u)
        o_ref[r] = (x * lax.rsqrt(power + 1e-06)[None]).astype(jnp.bfloat16)


def whiten(spectra, special, hi, t):
    ins = [spectra] + ([special] if t == 0 else [])
    specs = [pl.BlockSpec((2, 4, 1, CH, W), lambda i, hi_ref: (0, i, t, 0, 0))]
    if t == 0:
        specs.append(pl.BlockSpec((2, CH, W), lambda i, hi_ref: (0, 0, 0)))
    return pl.pallas_call(
        functools.partial(whiten_kernel, t),
        grid_spec=pltpu.PrefetchScalarGridSpec(
            num_scalar_prefetch=1,
            grid=(2,),
            in_specs=specs,
            out_specs=pl.BlockSpec((8, 2, CH, W), lambda i, hi_ref: (0, 0, 0, 0)),
        ),
        out_shape=jax.ShapeDtypeStruct((8, 2, CH, W), jnp.bfloat16),
        compiler_params=pltpu.CompilerParams(vmem_limit_bytes=VMEM),
        cost_estimate=pl.CostEstimate(flops=2000000, bytes_accessed=1 << 20, transcendentals=0),
        name="whiten",
    )(hi, *ins)


def plane(s, zpos):
    dist = lax.div(s + 1, 2)
    return lax.rem(zpos + 8 + jnp.where(lax.rem(s, 2) == 1, -dist, dist), 8)


def cross_kernel(first, count, z_ref, coef_ref, *refs):
    has_own = first == 0
    own, rest = refs[0:2], refs[2:]
    lows, highs = rest[:count - has_own], rest[count - has_own:2 * (count - has_own)]
    out_ref, left, base, bufs, outs, base_sem, in_sem, out_sem = refs[-8:]

    def load(j, side):
        src = (lows, highs)[side][j]
        return pltpu.make_async_copy(src, bufs.at[j, side], in_sem.at[j, side])

    def load_own(side):
        return pltpu.make_async_copy(own[side], base.at[side], base_sem.at[side])

    for side in range(2):
        load_own(side).start()
    for j in range(count - has_own):
        for side in range(2):
            load(j, side).start()
    for side in range(2):
        load_own(side).wait()
        re = base[side, :, 0].reshape(COLS, W).astype(jnp.float32)
        im = base[side, :, 1].reshape(COLS, W).astype(jnp.float32)
        for o in range(2):
            alpha = coef_ref[o * 4 + side * 2]
            beta = coef_ref[o * 4 + side * 2 + 1]
            rows = pl.ds(o * COLS, COLS)
            left[rows, side * 2 * W:side * 2 * W + W] = (alpha * re + beta * im).astype(jnp.bfloat16)
            left[rows, side * 2 * W + W:side * 2 * W + 2 * W] = (
                alpha * im - beta * re
            ).astype(jnp.bfloat16)

    def store(j):
        g = plane(j + first, z_ref[0])
        return pltpu.make_async_copy(outs.at[j], out_ref.at[g], out_sem.at[j])

    def emit(block, j):
        right = jnp.concatenate(
            [block[side, :, p].reshape(COLS, W) for side in range(2) for p in range(2)], axis=1
        )
        acc = lax.dot_general(
            left[...], right, (((1,), (1,)), ((), ())), preferred_element_type=jnp.float32
        )
        acc = (acc * (1.0 / W)).astype(jnp.bfloat16)
        for o in range(2):
            outs[j, :, o] = acc[o * COLS:(o + 1) * COLS].reshape(NQ, CH, COLS)
        store(j).start()

    if has_own:
        emit(base, 0)

    def body(j, carry):
        for side in range(2):
            pltpu.make_async_copy(own[0], bufs.at[j, side], in_sem.at[j, side]).wait()
        emit(bufs.at[j], j + has_own)
        return carry

    lax.fori_loop(0, count - has_own, body, 0)
    for j in range(count):
        store(j).wait()


def cross(zpos, coef, own, lows, highs, first, prev=None, flops=1 << 30):
    count = len(lows) + (first == 0)
    ins = [*own, *lows, *highs] + ([prev] if prev is not None else [])
    block = (NQ, 2, CH, W)
    return pl.pallas_call(
        functools.partial(cross_kernel, first, count),
        grid_spec=pltpu.PrefetchScalarGridSpec(
            num_scalar_prefetch=2,
            grid=(1,),
            in_specs=[pl.BlockSpec(memory_space=pl.ANY) for b in ins],
            out_specs=pl.BlockSpec(memory_space=pl.ANY),
            scratch_shapes=[
                pltpu.VMEM((2 * COLS, 4 * W), jnp.bfloat16),
                pltpu.VMEM((2, *block), jnp.bfloat16),
                pltpu.VMEM((len(lows), 2, *block), jnp.bfloat16),
                pltpu.VMEM((count, NQ, 2, CH, COLS), jnp.bfloat16),
                pltpu.SemaphoreType.DMA((2,)),
                pltpu.SemaphoreType.DMA((len(lows), 2)),
                pltpu.SemaphoreType.DMA((count,)),
            ],
        ),
        out_shape=jax.ShapeDtypeStruct((NK, NQ, 2, CH, COLS), jnp.bfloat16),
        input_output_aliases={} if prev is None else {len(ins) + 1: 0},
        compiler_params=pltpu.CompilerParams(vmem_limit_bytes=VMEM),
        cost_estimate=pl.CostEstimate(flops=flops, bytes_accessed=4 << 20, transcendentals=0),
        name="cross",
    )(zpos, coef, *ins)


def lags_kernel(t_ref, x1_ref, x0_ref, out_ref):
    x = jnp.concatenate([r[...].reshape(NK * NQ * 2, ROWS, COLS) for r in (x1_ref, x0_ref)])
    x = x.reshape(NK * NQ * 4, ROWS * COLS)
    y = jnp.dot(t_ref[...], x, preferred_element_type=jnp.float32) * math.sqrt(W / NF)
    out_ref[...] = y.reshape(LAGS, ROWS, COLS)


def lags(table, moved):
    n = NK * NQ * 4
    part = pl.BlockSpec((NK * NQ, 2, ROWS, COLS), lambda i: (0, 0, i, 0))
    return pl.pallas_call(
        lags_kernel,
        grid=(CH // ROWS,),
        in_specs=[pl.BlockSpec((LAGS, n), lambda i: (0, 0)), part, part],
        out_specs=pl.BlockSpec((LAGS, ROWS, COLS), lambda i: (0, i, 0)),
        out_shape=jax.ShapeDtypeStruct((LAGS, CH, COLS), jnp.float32),
        compiler_params=pltpu.CompilerParams(vmem_limit_bytes=VMEM),
        cost_estimate=pl.CostEstimate(flops=1 << 29, bytes_accessed=12 << 20, transcendentals=0),
        name="lags",
    )(table, *moved)


def shards(spectra):
    k = lax.axis_index("yh") * X + lax.axis_index("x")
    q = lax.axis_index("yl") * CO + lax.axis_index("co")
    hi = (k > 3).astype(jnp.int32).reshape(1)
    zpos = lax.axis_index("z").astype(jnp.int32).reshape(1)

    special = lax.ppermute(spectra[:, 0], ("yh", "x"), [(1, 0), (2, 1), (3, 2), (0, 3)])
    groups = [[j * NQ + i for j in (g, 7 - g) for i in range(NQ)] for g in range(4)]
    split = spectra.reshape(2, 8, 2, CH, W)

    white = {t: whiten(split, special, hi, t) for t in (1, 0)}

    def regroup(t):
        got = lax.all_to_all(
            white[t],
            PLANE, split_axis=0, concat_axis=0, tiled=True, axis_index_groups=groups,
        )
        return got[:NQ], got[NQ:]

    sin0 = -math.sin(0.0)
    sin64 = -math.sin(math.pi)
    regular = np.array([1, 0, 1, 0, 0, 1, 0, -1], np.float32)
    selfs = np.array([1, sin0, 0, 0, 0, 0, 1, sin64], np.float32)
    is_self = jnp.logical_and(k == 3, q == 0)
    coefs = {0: jnp.where(is_self, selfs, regular), 1: jnp.asarray(regular)}

    up = [(i, (i + 1) % Z) for i in range(Z)]
    dn = [((i + 1) % Z, i) for i in range(Z)]

    def ring(own):
        ups, dns = ([], []), ([], [])
        for s in range(4):
            for side in range(2):
                if s < 3 or side == 0:
                    ups[side].append(lax.ppermute(ups[side][-1] if s else own[side], "z", up))
                if s < 3 or side == 1:
                    dns[side].append(lax.ppermute(dns[side][-1] if s else own[side], "z", dn))
        return ups, dns

    table = jnp.asarray(lag_matrix())
    owns = {t: regroup(t) for t in (1, 0)}
    moved = []
    for t in (1, 0):
        own = owns[t]
        if t == 1:
            own, _ = lax.optimization_barrier((own, white[0]))
        else:
            own, _ = lax.optimization_barrier((own, (ups[1][2], near_parts)))
        ups, dns = ring(own)
        near = [(ups[i][s] if d == 0 else dns[i][s]) for i in range(2) for s in range(2) for d in range(2)]
        near_parts = parts = cross(zpos, coefs[t], own, near[:4], near[4:], 0)
        far = ([ups[0][2], dns[0][2], ups[0][3]], [ups[1][2], dns[1][2], dns[1][3]])
        parts = cross(zpos, coefs[t], own, *far, 5, parts, FLOPS if t == 0 else 1 << 29)
        parts = parts.reshape(NK * NQ, 2, CH, COLS)
        moved.append(lax.all_to_all(parts, PLANE, split_axis=0, concat_axis=0, tiled=True))
    return lags(table, moved)


def solution(mesh):
    fine = Mesh(mesh.devices.reshape(YH, X, Z, YL, CO), ("yh", "x", "z", "yl", "co"))
    return jax.shard_map(
        shards,
        mesh=fine,
        in_specs=(P(None, ("yh", "x"), ("z", "yl", "co"), None),),
        out_specs=P(None, ("z", "yl", "co"), ("yh", "x")),
        check_vma=False,
    )
```

```python
import functools
import math

import jax
import jax.numpy as jnp
import ml_dtypes
import numpy as np
from jax import lax
from jax.experimental import pallas as pl
from jax.experimental.pallas import tpu as pltpu
from jax.sharding import Mesh, PartitionSpec as P

LAGS = 128
NF = 128
W = 256
CH = 64
COLS = 256
X, YH, Z, YL, CO = 4, 2, 8, 2, 2
NK = YH * X
NQ = YL * CO
PLANE = ("yh", "x", "yl", "co")
VMEM = 20 * 1024 * 1024
ROWS = 32
FLOPS = 3 << 32


def lag_matrix():
    out = np.zeros((LAGS, 2, NK, NQ, 2), np.float32)
    lags = np.arange(LAGS)
    step = np.float32(2.0 * math.pi / LAGS)

    def angle(f):
        return step * (lags * f % LAGS).astype(np.float32)

    for k in range(NK):
        group, side = min(k, 7 - k), int(k > 3)
        for q in range(NQ):
            for t in range(2):
                m = 2 * (side * NQ + q) + t
                if m == 0 and group == 3:
                    out[:, t, k, q, 0] = np.cos(angle(0))
                    out[:, t, k, q, 1] = np.cos(angle(64))
                else:
                    f = 16 * group + m if m else 16 * (group + 1)
                    out[:, t, k, q, 0] = np.cos(angle(f))
                    out[:, t, k, q, 1] = -np.sin(angle(f))
    return out[:, ::-1].reshape(LAGS, NK * NQ * 4).astype(ml_dtypes.bfloat16)


def whiten_kernel(t, hi_ref, x_ref, *refs):
    o_ref = refs[-1]
    hi = hi_ref[0] == 1
    for j in range(4):
        u = pl.program_id(0) * 4 + j
        x = x_ref[:, j, 0].astype(jnp.float32)
        if t == 0 and j == 0:
            take = jnp.logical_and(jnp.logical_not(hi), pl.program_id(0) == 0)
            x = jnp.where(take, refs[0][...].astype(jnp.float32), x)
        power = jnp.sum(x[0] * x[0] + x[1] * x[1], axis=-1, keepdims=True) * (1.0 / W)
        r = jnp.where(hi, 7 - u if t else lax.rem(8 - u, 8), u)
        o_ref[r] = (x * lax.rsqrt(power + 1e-06)[None]).astype(jnp.bfloat16)


def whiten(spectra, special, hi, t):
    ins = [spectra] + ([special] if t == 0 else [])
    specs = [pl.BlockSpec((2, 4, 1, CH, W), lambda i, hi_ref: (0, i, t, 0, 0))]
    if t == 0:
        specs.append(pl.BlockSpec((2, CH, W), lambda i, hi_ref: (0, 0, 0)))
    return pl.pallas_call(
        functools.partial(whiten_kernel, t),
        grid_spec=pltpu.PrefetchScalarGridSpec(
            num_scalar_prefetch=1,
            grid=(2,),
            in_specs=specs,
            out_specs=pl.BlockSpec((8, 2, CH, W), lambda i, hi_ref: (0, 0, 0, 0)),
        ),
        out_shape=jax.ShapeDtypeStruct((8, 2, CH, W), jnp.bfloat16),
        compiler_params=pltpu.CompilerParams(vmem_limit_bytes=VMEM),
        cost_estimate=pl.CostEstimate(flops=2000000, bytes_accessed=1 << 20, transcendentals=0),
        name="whiten",
    )(hi, *ins)


def plane(s, zpos):
    dist = lax.div(s + 1, 2)
    return lax.rem(zpos + 8 + jnp.where(lax.rem(s, 2) == 1, -dist, dist), 8)


def cross_kernel(first, count, z_ref, coef_ref, *refs):
    has_own = first == 0
    own, rest = refs[0:2], refs[2:]
    lows, highs = rest[:count - has_own], rest[count - has_own:2 * (count - has_own)]
    out_ref, left, base, bufs, outs, base_sem, in_sem, out_sem = refs[-8:]

    def load(j, side):
        src = (lows, highs)[side][j]
        return pltpu.make_async_copy(src, bufs.at[j, side], in_sem.at[j, side])

    def load_own(side):
        return pltpu.make_async_copy(own[side], base.at[side], base_sem.at[side])

    for side in range(2):
        load_own(side).start()
    for j in range(count - has_own):
        for side in range(2):
            load(j, side).start()
    for side in range(2):
        load_own(side).wait()
        re = base[side, :, 0].reshape(COLS, W).astype(jnp.float32)
        im = base[side, :, 1].reshape(COLS, W).astype(jnp.float32)
        for o in range(2):
            alpha = coef_ref[o * 4 + side * 2]
            beta = coef_ref[o * 4 + side * 2 + 1]
            rows = pl.ds(o * COLS, COLS)
            left[rows, side * 2 * W:side * 2 * W + W] = (alpha * re + beta * im).astype(jnp.bfloat16)
            left[rows, side * 2 * W + W:side * 2 * W + 2 * W] = (
                alpha * im - beta * re
            ).astype(jnp.bfloat16)

    def store(j):
        g = plane(j + first, z_ref[0])
        return pltpu.make_async_copy(outs.at[j], out_ref.at[g], out_sem.at[j])

    def emit(block, j):
        right = jnp.concatenate(
            [block[side, :, p].reshape(COLS, W) for side in range(2) for p in range(2)], axis=1
        )
        acc = lax.dot_general(
            left[...], right, (((1,), (1,)), ((), ())), preferred_element_type=jnp.float32
        )
        acc = (acc * (1.0 / W)).astype(jnp.bfloat16)
        for o in range(2):
            outs[j, :, o] = acc[o * COLS:(o + 1) * COLS].reshape(NQ, CH, COLS)
        store(j).start()

    if has_own:
        emit(base, 0)

    def body(j, carry):
        for side in range(2):
            pltpu.make_async_copy(own[0], bufs.at[j, side], in_sem.at[j, side]).wait()
        emit(bufs.at[j], j + has_own)
        return carry

    lax.fori_loop(0, count - has_own, body, 0)
    for j in range(count):
        store(j).wait()


def cross(zpos, coef, own, lows, highs, first, prev=None, flops=1 << 30):
    count = len(lows) + (first == 0)
    ins = [*own, *lows, *highs] + ([prev] if prev is not None else [])
    block = (NQ, 2, CH, W)
    return pl.pallas_call(
        functools.partial(cross_kernel, first, count),
        grid_spec=pltpu.PrefetchScalarGridSpec(
            num_scalar_prefetch=2,
            grid=(1,),
            in_specs=[pl.BlockSpec(memory_space=pl.ANY) for b in ins],
            out_specs=pl.BlockSpec(memory_space=pl.ANY),
            scratch_shapes=[
                pltpu.VMEM((2 * COLS, 4 * W), jnp.bfloat16),
                pltpu.VMEM((2, *block), jnp.bfloat16),
                pltpu.VMEM((len(lows), 2, *block), jnp.bfloat16),
                pltpu.VMEM((count, NQ, 2, CH, COLS), jnp.bfloat16),
                pltpu.SemaphoreType.DMA((2,)),
                pltpu.SemaphoreType.DMA((len(lows), 2)),
                pltpu.SemaphoreType.DMA((count,)),
            ],
        ),
        out_shape=jax.ShapeDtypeStruct((NK, NQ, 2, CH, COLS), jnp.bfloat16),
        input_output_aliases={} if prev is None else {len(ins) + 1: 0},
        compiler_params=pltpu.CompilerParams(vmem_limit_bytes=VMEM),
        cost_estimate=pl.CostEstimate(flops=flops, bytes_accessed=4 << 20, transcendentals=0),
        name="cross",
    )(zpos, coef, *ins)


def lags_kernel(t_ref, x1_ref, x0_ref, out_ref):
    x = jnp.concatenate([r[...].reshape(NK * NQ * 2, ROWS, COLS) for r in (x1_ref, x0_ref)])
    x = x.reshape(NK * NQ * 4, ROWS * COLS)
    y = jnp.dot(t_ref[...], x, preferred_element_type=jnp.float32) * math.sqrt(W / NF)
    out_ref[...] = y.reshape(LAGS, ROWS, COLS)


def lags(table, moved):
    n = NK * NQ * 4
    part = pl.BlockSpec((NK * NQ, 2, ROWS, COLS), lambda i: (0, 0, i, 0))
    return pl.pallas_call(
        lags_kernel,
        grid=(CH // ROWS,),
        in_specs=[pl.BlockSpec((LAGS, n), lambda i: (0, 0)), part, part],
        out_specs=pl.BlockSpec((LAGS, ROWS, COLS), lambda i: (0, i, 0)),
        out_shape=jax.ShapeDtypeStruct((LAGS, CH, COLS), jnp.float32),
        compiler_params=pltpu.CompilerParams(vmem_limit_bytes=VMEM),
        cost_estimate=pl.CostEstimate(flops=1 << 29, bytes_accessed=12 << 20, transcendentals=0),
        name="lags",
    )(table, *moved)


def shards(spectra):
    k = lax.axis_index("yh") * X + lax.axis_index("x")
    q = lax.axis_index("yl") * CO + lax.axis_index("co")
    hi = (k > 3).astype(jnp.int32).reshape(1)
    zpos = lax.axis_index("z").astype(jnp.int32).reshape(1)

    special = lax.ppermute(spectra[:, 0], ("yh", "x"), [(1, 0), (2, 1), (3, 2), (0, 3)])
    groups = [[j * NQ + i for j in (g, 7 - g) for i in range(NQ)] for g in range(4)]
    split = spectra.reshape(2, 8, 2, CH, W)

    white = {t: whiten(split, special, hi, t) for t in (1, 0)}

    def regroup(t):
        got = lax.all_to_all(
            white[t],
            PLANE, split_axis=0, concat_axis=0, tiled=True, axis_index_groups=groups,
        )
        return got[:NQ], got[NQ:]

    sin0 = -math.sin(0.0)
    sin64 = -math.sin(math.pi)
    regular = np.array([1, 0, 1, 0, 0, 1, 0, -1], np.float32)
    selfs = np.array([1, sin0, 0, 0, 0, 0, 1, sin64], np.float32)
    is_self = jnp.logical_and(k == 3, q == 0)
    coefs = {0: jnp.where(is_self, selfs, regular), 1: jnp.asarray(regular)}

    up = [(i, (i + 1) % Z) for i in range(Z)]
    dn = [((i + 1) % Z, i) for i in range(Z)]

    def ring(own, before=None):
        ups, dns = ([], []), ([], [])
        for s in range(4):
            if s == 1 and before is not None:
                ups, dns = jax.tree.map(lambda v: lax.optimization_barrier((v, before))[0], (ups, dns))
            for side in range(2):
                if s < 3 or side == 0:
                    ups[side].append(lax.ppermute(ups[side][-1] if s else own[side], "z", up))
                if s < 3 or side == 1:
                    dns[side].append(lax.ppermute(dns[side][-1] if s else own[side], "z", dn))
        return ups, dns

    table = jnp.asarray(lag_matrix())
    moved = []
    for t in (1, 0):
        if t == 1:
            own, _ = lax.optimization_barrier((regroup(t), white[0]))
        else:
            white[0], _ = lax.optimization_barrier((white[0], ups[0][0]))
            own = regroup(t)
            own, _ = lax.optimization_barrier((own, (ups[1][2], near_parts)))
        ups, dns = ring(own, parts if t == 0 else None)
        near = [(ups[i][s] if d == 0 else dns[i][s]) for i in range(2) for s in range(2) for d in range(2)]
        near_parts = parts = cross(zpos, coefs[t], own, near[:4], near[4:], 0)
        far = ([ups[0][2], dns[0][2], ups[0][3]], [ups[1][2], dns[1][2], dns[1][3]])
        parts = cross(zpos, coefs[t], own, *far, 5, parts, FLOPS if t == 0 else 1 << 29)
        parts = parts.reshape(NK * NQ, 2, CH, COLS)
        moved.append(lax.all_to_all(parts, PLANE, split_axis=0, concat_axis=0, tiled=True))
    return lags(table, moved)


def solution(mesh):
    fine = Mesh(mesh.devices.reshape(YH, X, Z, YL, CO), ("yh", "x", "z", "yl", "co"))
    return jax.shard_map(
        shards,
        mesh=fine,
        in_specs=(P(None, ("yh", "x"), ("z", "yl", "co"), None),),
        out_specs=P(None, ("z", "yl", "co"), ("yh", "x")),
        check_vma=False,
    )
```

```python
import functools
import math

import jax
import jax.numpy as jnp
import ml_dtypes
import numpy as np
from jax import lax
from jax.experimental import pallas as pl
from jax.experimental.pallas import tpu as pltpu
from jax.sharding import Mesh, PartitionSpec as P

LAGS = 128
NF = 128
W = 256
CH = 64
COLS = 256
X, YH, Z, YL, CO = 4, 2, 8, 2, 2
NK = YH * X
NQ = YL * CO
PLANE = ("yh", "x", "yl", "co")
VMEM = 20 * 1024 * 1024
ROWS = 32
FLOPS = 3 << 32


def lag_matrix():
    out = np.zeros((LAGS, 2, NK, NQ, 2), np.float32)
    lags = np.arange(LAGS)
    step = np.float32(2.0 * math.pi / LAGS)

    def angle(f):
        return step * (lags * f % LAGS).astype(np.float32)

    for k in range(NK):
        group, side = min(k, 7 - k), int(k > 3)
        for q in range(NQ):
            for t in range(2):
                m = 2 * (side * NQ + q) + t
                if m == 0 and group == 3:
                    out[:, t, k, q, 0] = np.cos(angle(0))
                    out[:, t, k, q, 1] = np.cos(angle(64))
                else:
                    f = 16 * group + m if m else 16 * (group + 1)
                    out[:, t, k, q, 0] = np.cos(angle(f))
                    out[:, t, k, q, 1] = -np.sin(angle(f))
    return out[:, ::-1].reshape(LAGS, NK * NQ * 4).astype(ml_dtypes.bfloat16)


def whiten_kernel(t, hi_ref, x_ref, *refs):
    o_ref = refs[-1]
    hi = hi_ref[0] == 1
    for j in range(4):
        u = pl.program_id(0) * 4 + j
        x = x_ref[:, j, 0].astype(jnp.float32)
        if t == 0 and j == 0:
            take = jnp.logical_and(jnp.logical_not(hi), pl.program_id(0) == 0)
            x = jnp.where(take, refs[0][...].astype(jnp.float32), x)
        power = jnp.sum(x[0] * x[0] + x[1] * x[1], axis=-1, keepdims=True) * (1.0 / W)
        if t:
            r = jnp.where(hi, 3 - j, j)
        else:
            r = jnp.where(hi, lax.rem(8 - u, 8), u)
        o_ref[r] = (x * lax.rsqrt(power + 1e-06)[None]).astype(jnp.bfloat16)


def whiten(spectra, special, hi, t):
    ins = [spectra] + ([special] if t == 0 else [])
    specs = [pl.BlockSpec((2, 4, 1, CH, W), lambda i, hi_ref: (0, i, t, 0, 0))]
    if t == 0:
        specs.append(pl.BlockSpec((2, CH, W), lambda i, hi_ref: (0, 0, 0)))
    if t:
        half = lambda i, hi_ref: (jnp.where(hi_ref[0] == 1, 1 - i, i), 0, 0, 0)
        out_spec = pl.BlockSpec((4, 2, CH, W), half)
    else:
        out_spec = pl.BlockSpec((8, 2, CH, W), lambda i, hi_ref: (0, 0, 0, 0))
    return pl.pallas_call(
        functools.partial(whiten_kernel, t),
        grid_spec=pltpu.PrefetchScalarGridSpec(
            num_scalar_prefetch=1,
            grid=(2,),
            in_specs=specs,
            out_specs=out_spec,
        ),
        out_shape=jax.ShapeDtypeStruct((8, 2, CH, W), jnp.bfloat16),
        compiler_params=pltpu.CompilerParams(vmem_limit_bytes=56 * 1024 * 1024),
        cost_estimate=pl.CostEstimate(flops=2000000, bytes_accessed=1 << 20, transcendentals=0),
        name="whiten",
    )(hi, *ins)


def plane(s, zpos):
    dist = lax.div(s + 1, 2)
    return lax.rem(zpos + 8 + jnp.where(lax.rem(s, 2) == 1, -dist, dist), 8)


def cross_kernel(first, count, z_ref, coef_ref, *refs):
    has_own = first == 0
    own, rest = refs[0:2], refs[2:]
    lows, highs = rest[:count - has_own], rest[count - has_own:2 * (count - has_own)]
    out_ref, left, base, bufs, outs, base_sem, in_sem, out_sem = refs[-8:]

    def load(j, side):
        src = (lows, highs)[side][j]
        return pltpu.make_async_copy(src, bufs.at[j, side], in_sem.at[j, side])

    def load_own(side):
        return pltpu.make_async_copy(own[side], base.at[side], base_sem.at[side])

    for side in range(2):
        load_own(side).start()
    for j in range(count - has_own):
        for side in range(2):
            load(j, side).start()
    for side in range(2):
        load_own(side).wait()
        re = base[side, :, 0].reshape(COLS, W).astype(jnp.float32)
        im = base[side, :, 1].reshape(COLS, W).astype(jnp.float32)
        for o in range(2):
            alpha = coef_ref[o * 4 + side * 2]
            beta = coef_ref[o * 4 + side * 2 + 1]
            rows = pl.ds(o * COLS, COLS)
            left[rows, side * 2 * W:side * 2 * W + W] = (alpha * re + beta * im).astype(jnp.bfloat16)
            left[rows, side * 2 * W + W:side * 2 * W + 2 * W] = (
                alpha * im - beta * re
            ).astype(jnp.bfloat16)

    def store(j):
        g = plane(j + first, z_ref[0])
        return pltpu.make_async_copy(outs.at[j], out_ref.at[g], out_sem.at[j])

    def emit(block, j):
        right = jnp.concatenate(
            [block[side, :, p].reshape(COLS, W) for side in range(2) for p in range(2)], axis=1
        )
        acc = lax.dot_general(
            left[...], right, (((1,), (1,)), ((), ())), preferred_element_type=jnp.float32
        )
        acc = (acc * (1.0 / W)).astype(jnp.bfloat16)
        for o in range(2):
            outs[j, :, o] = acc[o * COLS:(o + 1) * COLS].reshape(NQ, CH, COLS)
        store(j).start()

    if has_own:
        emit(base, 0)

    def body(j, carry):
        for side in range(2):
            pltpu.make_async_copy(own[0], bufs.at[j, side], in_sem.at[j, side]).wait()
        emit(bufs.at[j], j + has_own)
        return carry

    lax.fori_loop(0, count - has_own, body, 0)
    for j in range(count):
        store(j).wait()


def cross(zpos, coef, own, lows, highs, first, prev=None, flops=1 << 30):
    count = len(lows) + (first == 0)
    ins = [*own, *lows, *highs] + ([prev] if prev is not None else [])
    block = (NQ, 2, CH, W)
    return pl.pallas_call(
        functools.partial(cross_kernel, first, count),
        grid_spec=pltpu.PrefetchScalarGridSpec(
            num_scalar_prefetch=2,
            grid=(1,),
            in_specs=[pl.BlockSpec(memory_space=pl.ANY) for b in ins],
            out_specs=pl.BlockSpec(memory_space=pl.ANY),
            scratch_shapes=[
                pltpu.VMEM((2 * COLS, 4 * W), jnp.bfloat16),
                pltpu.VMEM((2, *block), jnp.bfloat16),
                pltpu.VMEM((len(lows), 2, *block), jnp.bfloat16),
                pltpu.VMEM((count, NQ, 2, CH, COLS), jnp.bfloat16),
                pltpu.SemaphoreType.DMA((2,)),
                pltpu.SemaphoreType.DMA((len(lows), 2)),
                pltpu.SemaphoreType.DMA((count,)),
            ],
        ),
        out_shape=jax.ShapeDtypeStruct((NK, NQ, 2, CH, COLS), jnp.bfloat16),
        input_output_aliases={} if prev is None else {len(ins) + 1: 0},
        compiler_params=pltpu.CompilerParams(vmem_limit_bytes=VMEM),
        cost_estimate=pl.CostEstimate(flops=flops, bytes_accessed=4 << 20, transcendentals=0),
        name="cross",
    )(zpos, coef, *ins)


def lags_kernel(t_ref, x1_ref, x0_ref, out_ref):
    x = jnp.concatenate([r[...].reshape(NK * NQ * 2, ROWS, COLS) for r in (x1_ref, x0_ref)])
    x = x.reshape(NK * NQ * 4, ROWS * COLS)
    y = jnp.dot(t_ref[...], x, preferred_element_type=jnp.float32) * math.sqrt(W / NF)
    out_ref[...] = y.reshape(LAGS, ROWS, COLS)


def lags(table, moved):
    n = NK * NQ * 4
    part = pl.BlockSpec((NK * NQ, 2, ROWS, COLS), lambda i: (0, 0, i, 0))
    return pl.pallas_call(
        lags_kernel,
        grid=(CH // ROWS,),
        in_specs=[pl.BlockSpec((LAGS, n), lambda i: (0, 0)), part, part],
        out_specs=pl.BlockSpec((LAGS, ROWS, COLS), lambda i: (0, i, 0)),
        out_shape=jax.ShapeDtypeStruct((LAGS, CH, COLS), jnp.float32),
        compiler_params=pltpu.CompilerParams(vmem_limit_bytes=VMEM),
        cost_estimate=pl.CostEstimate(flops=1 << 29, bytes_accessed=12 << 20, transcendentals=0),
        name="lags",
    )(table, *moved)


def shards(spectra):
    k = lax.axis_index("yh") * X + lax.axis_index("x")
    q = lax.axis_index("yl") * CO + lax.axis_index("co")
    hi = (k > 3).astype(jnp.int32).reshape(1)
    zpos = lax.axis_index("z").astype(jnp.int32).reshape(1)

    special = lax.ppermute(spectra[:, 0], ("yh", "x"), [(1, 0), (2, 1), (3, 2), (0, 3)])
    groups = [[j * NQ + i for j in (g, 7 - g) for i in range(NQ)] for g in range(4)]
    split = spectra.reshape(2, 8, 2, CH, W)

    white = {t: whiten(split, special, hi, t) for t in (1, 0)}

    def regroup(t):
        got = lax.all_to_all(
            white[t],
            PLANE, split_axis=0, concat_axis=0, tiled=True, axis_index_groups=groups,
        )
        return got[:NQ], got[NQ:]

    sin0 = -math.sin(0.0)
    sin64 = -math.sin(math.pi)
    regular = np.array([1, 0, 1, 0, 0, 1, 0, -1], np.float32)
    selfs = np.array([1, sin0, 0, 0, 0, 0, 1, sin64], np.float32)
    is_self = jnp.logical_and(k == 3, q == 0)
    coefs = {0: jnp.where(is_self, selfs, regular), 1: jnp.asarray(regular)}

    up = [(i, (i + 1) % Z) for i in range(Z)]
    dn = [((i + 1) % Z, i) for i in range(Z)]

    def ring(own, before=None, t=0):
        ups, dns = ([], []), ([], [])
        for s in range(4):
            if s == 3:
                near = [(ups[i][n] if d == 0 else dns[i][n]) for i in range(2) for n in range(2) for d in range(2)]
                near_parts = cross(zpos, coefs[t], own, near[:4], near[4:], 0)
                if True:
                    ups, dns = [list(v) for v in ups], [list(v) for v in dns]
                    ups[0][2], dns[1][2], _ = lax.optimization_barrier((ups[0][2], dns[1][2], near_parts))
            if s == 1 and before is not None:
                ups, dns = jax.tree.map(lambda v: lax.optimization_barrier((v, before))[0], (ups, dns))
            for side in range(2):
                if s < 3 or side == 0:
                    ups[side].append(lax.ppermute(ups[side][-1] if s else own[side], "z", up))
                if s < 3 or side == 1:
                    dns[side].append(lax.ppermute(dns[side][-1] if s else own[side], "z", dn))
        return ups, dns, near_parts

    table = jnp.asarray(lag_matrix())
    moved = []
    for t in (1, 0):
        if t == 1:
            own, _ = lax.optimization_barrier((regroup(t), white[0]))
        else:
            white[0], _ = lax.optimization_barrier((white[0], ups[0][0]))
            own = regroup(t)
            own, _ = lax.optimization_barrier((own, ups[1][2]))
        ups, dns, near_parts = ring(own, parts if t == 0 else None, t)
        parts = near_parts
        far = ([ups[0][2], dns[0][2], ups[0][3]], [ups[1][2], dns[1][2], dns[1][3]])
        parts = cross(zpos, coefs[t], own, *far, 5, parts, FLOPS if t == 0 else 1 << 29)
        parts = parts.reshape(NK * NQ, 2, CH, COLS)
        moved.append(lax.all_to_all(parts, PLANE, split_axis=0, concat_axis=0, tiled=True))
    return lags(table, moved)


def solution(mesh):
    fine = Mesh(mesh.devices.reshape(YH, X, Z, YL, CO), ("yh", "x", "z", "yl", "co"))
    return jax.shard_map(
        shards,
        mesh=fine,
        in_specs=(P(None, ("yh", "x"), ("z", "yl", "co"), None),),
        out_specs=P(None, ("z", "yl", "co"), ("yh", "x")),
        check_vma=False,
    )
```

```python
import functools
import math

import jax
import jax.numpy as jnp
import ml_dtypes
import numpy as np
from jax import lax
from jax.experimental import pallas as pl
from jax.experimental.pallas import tpu as pltpu
from jax.sharding import Mesh, PartitionSpec as P

LAGS = 128
NF = 128
W = 256
CH = 64
COLS = 256
X, YH, Z, YL, CO = 4, 2, 8, 2, 2
NK = YH * X
NQ = YL * CO
PLANE = ("yh", "x", "yl", "co")
VMEM = 20 * 1024 * 1024
ROWS = 16
FLOPS = 3 << 32


def lag_matrix():
    out = np.zeros((LAGS, 2, NK, NQ, 2), np.float32)
    lags = np.arange(LAGS)
    step = np.float32(2.0 * math.pi / LAGS)

    def angle(f):
        return step * (lags * f % LAGS).astype(np.float32)

    for k in range(NK):
        group, side = min(k, 7 - k), int(k > 3)
        for q in range(NQ):
            for t in range(2):
                m = 2 * (side * NQ + q) + t
                if m == 0 and group == 3:
                    out[:, t, k, q, 0] = np.cos(angle(0))
                    out[:, t, k, q, 1] = np.cos(angle(64))
                else:
                    f = 16 * group + m if m else 16 * (group + 1)
                    out[:, t, k, q, 0] = np.cos(angle(f))
                    out[:, t, k, q, 1] = -np.sin(angle(f))
    return out[:, ::-1].reshape(LAGS, NK * NQ * 4).astype(ml_dtypes.bfloat16)


def whiten_kernel(t, hi_ref, x_ref, *refs):
    o_ref = refs[-1]
    hi = hi_ref[0] == 1
    for j in range(4):
        u = pl.program_id(0) * 4 + j
        x = x_ref[:, j, 0].astype(jnp.float32)
        if t == 0 and j == 0:
            take = jnp.logical_and(jnp.logical_not(hi), pl.program_id(0) == 0)
            x = jnp.where(take, refs[0][...].astype(jnp.float32), x)
        power = jnp.sum(x[0] * x[0] + x[1] * x[1], axis=-1, keepdims=True) * (1.0 / W)
        if t:
            r = jnp.where(hi, 3 - j, j)
        else:
            r = jnp.where(hi, lax.rem(8 - u, 8), u)
        o_ref[r] = (x * lax.rsqrt(power + 1e-06)[None]).astype(jnp.bfloat16)


def whiten(spectra, special, hi, t):
    ins = [spectra] + ([special] if t == 0 else [])
    specs = [pl.BlockSpec((2, 4, 1, CH, W), lambda i, hi_ref: (0, i, t, 0, 0))]
    if t == 0:
        specs.append(pl.BlockSpec((2, CH, W), lambda i, hi_ref: (0, 0, 0)))
    if t:
        half = lambda i, hi_ref: (jnp.where(hi_ref[0] == 1, 1 - i, i), 0, 0, 0)
        out_spec = pl.BlockSpec((4, 2, CH, W), half)
    else:
        out_spec = pl.BlockSpec((8, 2, CH, W), lambda i, hi_ref: (0, 0, 0, 0))
    return pl.pallas_call(
        functools.partial(whiten_kernel, t),
        grid_spec=pltpu.PrefetchScalarGridSpec(
            num_scalar_prefetch=1,
            grid=(2,),
            in_specs=specs,
            out_specs=out_spec,
        ),
        out_shape=jax.ShapeDtypeStruct((8, 2, CH, W), jnp.bfloat16),
        compiler_params=pltpu.CompilerParams(vmem_limit_bytes=56 * 1024 * 1024),
        cost_estimate=pl.CostEstimate(flops=2000000, bytes_accessed=1 << 20, transcendentals=0),
        name="whiten",
    )(hi, *ins)


def plane(s, zpos):
    dist = lax.div(s + 1, 2)
    return lax.rem(zpos + 8 + jnp.where(lax.rem(s, 2) == 1, -dist, dist), 8)


def cross_kernel(first, count, z_ref, coef_ref, *refs):
    has_own = first == 0
    own, rest = refs[0:2], refs[2:]
    lows, highs = rest[:count - has_own], rest[count - has_own:2 * (count - has_own)]
    out_ref, left, base, bufs, outs, base_sem, in_sem, out_sem = refs[-8:]

    def load(j, side):
        src = (lows, highs)[side][j]
        return pltpu.make_async_copy(src, bufs.at[j, side], in_sem.at[j, side])

    def load_own(side):
        return pltpu.make_async_copy(own[side], base.at[side], base_sem.at[side])

    for side in range(2):
        load_own(side).start()
    for j in range(count - has_own):
        for side in range(2):
            load(j, side).start()
    for side in range(2):
        load_own(side).wait()
        re = base[side, :, 0].reshape(COLS, W).astype(jnp.float32)
        im = base[side, :, 1].reshape(COLS, W).astype(jnp.float32)
        for o in range(2):
            alpha = coef_ref[o * 4 + side * 2]
            beta = coef_ref[o * 4 + side * 2 + 1]
            rows = pl.ds(o * COLS, COLS)
            left[rows, side * 2 * W:side * 2 * W + W] = (alpha * re + beta * im).astype(jnp.bfloat16)
            left[rows, side * 2 * W + W:side * 2 * W + 2 * W] = (
                alpha * im - beta * re
            ).astype(jnp.bfloat16)

    def store(j):
        g = plane(j + first, z_ref[0])
        return pltpu.make_async_copy(outs.at[j], out_ref.at[g], out_sem.at[j])

    def emit(block, j):
        right = jnp.concatenate(
            [block[side, :, p].reshape(COLS, W) for side in range(2) for p in range(2)], axis=1
        )
        acc = lax.dot_general(
            left[...], right, (((1,), (1,)), ((), ())), preferred_element_type=jnp.float32
        )
        acc = (acc * (1.0 / W)).astype(jnp.bfloat16)
        for o in range(2):
            outs[j, :, o] = acc[o * COLS:(o + 1) * COLS].reshape(NQ, CH, COLS)
        store(j).start()

    if has_own:
        emit(base, 0)

    def body(j, carry):
        for side in range(2):
            pltpu.make_async_copy(own[0], bufs.at[j, side], in_sem.at[j, side]).wait()
        emit(bufs.at[j], j + has_own)
        return carry

    lax.fori_loop(0, count - has_own, body, 0)
    for j in range(count):
        store(j).wait()


def cross(zpos, coef, own, lows, highs, first, prev=None, flops=1 << 30):
    count = len(lows) + (first == 0)
    ins = [*own, *lows, *highs] + ([prev] if prev is not None else [])
    block = (NQ, 2, CH, W)
    return pl.pallas_call(
        functools.partial(cross_kernel, first, count),
        grid_spec=pltpu.PrefetchScalarGridSpec(
            num_scalar_prefetch=2,
            grid=(1,),
            in_specs=[pl.BlockSpec(memory_space=pl.ANY) for b in ins],
            out_specs=pl.BlockSpec(memory_space=pl.ANY),
            scratch_shapes=[
                pltpu.VMEM((2 * COLS, 4 * W), jnp.bfloat16),
                pltpu.VMEM((2, *block), jnp.bfloat16),
                pltpu.VMEM((len(lows), 2, *block), jnp.bfloat16),
                pltpu.VMEM((count, NQ, 2, CH, COLS), jnp.bfloat16),
                pltpu.SemaphoreType.DMA((2,)),
                pltpu.SemaphoreType.DMA((len(lows), 2)),
                pltpu.SemaphoreType.DMA((count,)),
            ],
        ),
        out_shape=jax.ShapeDtypeStruct((NK, NQ, 2, CH, COLS), jnp.bfloat16),
        input_output_aliases={} if prev is None else {len(ins) + 1: 0},
        compiler_params=pltpu.CompilerParams(vmem_limit_bytes=VMEM),
        cost_estimate=pl.CostEstimate(flops=flops, bytes_accessed=4 << 20, transcendentals=0),
        name="cross",
    )(zpos, coef, *ins)


def arrange_kernel(x_ref, o_ref):
    o_ref[0] = x_ref[...].reshape(o_ref.shape[1:])


def arrange(moved):
    n = NK * NQ * 2
    return pl.pallas_call(
        arrange_kernel,
        grid=(CH // ROWS,),
        in_specs=[pl.BlockSpec((n, ROWS, COLS), lambda i: (0, i, 0))],
        out_specs=pl.BlockSpec((1, n, ROWS * COLS), lambda i: (i, 0, 0)),
        out_shape=jax.ShapeDtypeStruct((CH // ROWS, n, ROWS * COLS), jnp.bfloat16),
        compiler_params=pltpu.CompilerParams(vmem_limit_bytes=VMEM),
        cost_estimate=pl.CostEstimate(flops=1 << 20, bytes_accessed=4 << 20, transcendentals=0),
        name="arrange",
    )(moved.reshape(n, CH, COLS))


def lags_kernel(t_ref, x1_ref, x0_ref, out_ref):
    x = jnp.concatenate([x1_ref[0], x0_ref[...].reshape(NK * NQ * 2, ROWS * COLS)])
    y = jnp.dot(t_ref[...], x, preferred_element_type=jnp.float32) * math.sqrt(W / NF)
    out_ref[...] = y.reshape(LAGS, ROWS, COLS)


def lags(table, first, second):
    n = NK * NQ * 2
    return pl.pallas_call(
        lags_kernel,
        grid=(CH // ROWS,),
        in_specs=[
            pl.BlockSpec((LAGS, 2 * n), lambda i: (0, 0)),
            pl.BlockSpec((1, n, ROWS * COLS), lambda i: (i, 0, 0)),
            pl.BlockSpec((n, ROWS, COLS), lambda i: (0, i, 0)),
        ],
        out_specs=pl.BlockSpec((LAGS, ROWS, COLS), lambda i: (0, i, 0)),
        out_shape=jax.ShapeDtypeStruct((LAGS, CH, COLS), jnp.float32),
        compiler_params=pltpu.CompilerParams(vmem_limit_bytes=VMEM),
        cost_estimate=pl.CostEstimate(flops=1 << 29, bytes_accessed=12 << 20, transcendentals=0),
        name="lags",
    )(table, first, second.reshape(n, CH, COLS))


def shards(spectra):
    k = lax.axis_index("yh") * X + lax.axis_index("x")
    q = lax.axis_index("yl") * CO + lax.axis_index("co")
    hi = (k > 3).astype(jnp.int32).reshape(1)
    zpos = lax.axis_index("z").astype(jnp.int32).reshape(1)

    special = lax.ppermute(spectra[:, 0], ("yh", "x"), [(1, 0), (2, 1), (3, 2), (0, 3)])
    groups = [[j * NQ + i for j in (g, 7 - g) for i in range(NQ)] for g in range(4)]
    split = spectra.reshape(2, 8, 2, CH, W)

    white = {t: whiten(split, special, hi, t) for t in (1, 0)}

    def regroup(t):
        got = lax.all_to_all(
            white[t],
            PLANE, split_axis=0, concat_axis=0, tiled=True, axis_index_groups=groups,
        )
        return got[:NQ], got[NQ:]

    sin0 = -math.sin(0.0)
    sin64 = -math.sin(math.pi)
    regular = np.array([1, 0, 1, 0, 0, 1, 0, -1], np.float32)
    selfs = np.array([1, sin0, 0, 0, 0, 0, 1, sin64], np.float32)
    is_self = jnp.logical_and(k == 3, q == 0)
    coefs = {0: jnp.where(is_self, selfs, regular), 1: jnp.asarray(regular)}

    up = [(i, (i + 1) % Z) for i in range(Z)]
    dn = [((i + 1) % Z, i) for i in range(Z)]

    def ring(own, before=None, t=0):
        ups, dns = ([], []), ([], [])
        for s in range(4):
            if s == 3:
                near = [(ups[i][n] if d == 0 else dns[i][n]) for i in range(2) for n in range(2) for d in range(2)]
                near_parts = cross(zpos, coefs[t], own, near[:4], near[4:], 0)
                if True:
                    ups, dns = [list(v) for v in ups], [list(v) for v in dns]
                    ups[0][2], dns[1][2], _ = lax.optimization_barrier((ups[0][2], dns[1][2], near_parts))
            if s == 1 and before is not None:
                ups, dns = jax.tree.map(lambda v: lax.optimization_barrier((v, before))[0], (ups, dns))
            for side in range(2):
                if s < 3 or side == 0:
                    ups[side].append(lax.ppermute(ups[side][-1] if s else own[side], "z", up))
                if s < 3 or side == 1:
                    dns[side].append(lax.ppermute(dns[side][-1] if s else own[side], "z", dn))
        return ups, dns, near_parts

    table = jnp.asarray(lag_matrix())
    moved = []
    for t in (1, 0):
        if t == 1:
            own, _ = lax.optimization_barrier((regroup(t), white[0]))
        else:
            white[0], _ = lax.optimization_barrier((white[0], ups[0][0]))
            own = regroup(t)
            own, _ = lax.optimization_barrier((own, ups[1][2]))
        ups, dns, near_parts = ring(own, parts if t == 0 else None, t)
        parts = near_parts
        far = ([ups[0][2], dns[0][2], ups[0][3]], [ups[1][2], dns[1][2], dns[1][3]])
        parts = cross(zpos, coefs[t], own, *far, 5, parts, FLOPS if t == 0 else 1 << 29)
        if t == 0:
            ready = arrange(moved[0])
            parts, ready = lax.optimization_barrier((parts, ready))
        parts = parts.reshape(NK * NQ, 2, CH, COLS)
        moved.append(lax.all_to_all(parts, PLANE, split_axis=0, concat_axis=0, tiled=True))
    return lags(table, ready, moved[1])


def solution(mesh):
    fine = Mesh(mesh.devices.reshape(YH, X, Z, YL, CO), ("yh", "x", "z", "yl", "co"))
    return jax.shard_map(
        shards,
        mesh=fine,
        in_specs=(P(None, ("yh", "x"), ("z", "yl", "co"), None),),
        out_specs=P(None, ("z", "yl", "co"), ("yh", "x")),
        check_vma=False,
    )
```

```python
import functools
import math

import jax
import jax.numpy as jnp
import ml_dtypes
import numpy as np
from jax import lax
from jax.experimental import pallas as pl
from jax.experimental.pallas import tpu as pltpu
from jax.sharding import Mesh, PartitionSpec as P

LAGS = 128
NF = 128
W = 256
CH = 64
COLS = 256
X, YH, Z, YL, CO = 4, 2, 8, 2, 2
NK = YH * X
NQ = YL * CO
PLANE = ("yh", "x", "yl", "co")
VMEM = 20 * 1024 * 1024
ROWS = 32
FLOPS = 3 << 32


def lag_matrix():
    out = np.zeros((LAGS, 2, NK, NQ, 2), np.float32)
    lags = np.arange(LAGS)
    step = np.float32(2.0 * math.pi / LAGS)

    def angle(f):
        return step * (lags * f % LAGS).astype(np.float32)

    for k in range(NK):
        group, side = min(k, 7 - k), int(k > 3)
        for q in range(NQ):
            for t in range(2):
                m = 2 * (side * NQ + q) + t
                if m == 0 and group == 3:
                    out[:, t, k, q, 0] = np.cos(angle(0))
                    out[:, t, k, q, 1] = np.cos(angle(64))
                else:
                    f = 16 * group + m if m else 16 * (group + 1)
                    out[:, t, k, q, 0] = np.cos(angle(f))
                    out[:, t, k, q, 1] = -np.sin(angle(f))
    return out[:, ::-1].reshape(LAGS, NK * NQ * 4).astype(ml_dtypes.bfloat16)


def whiten_kernel(t, hi_ref, x_ref, *refs):
    o_ref = refs[-1]
    hi = hi_ref[0] == 1
    for j in range(4):
        u = pl.program_id(0) * 4 + j
        x = x_ref[:, j, 0].astype(jnp.float32)
        if t == 0 and j == 0:
            take = jnp.logical_and(jnp.logical_not(hi), pl.program_id(0) == 0)
            x = jnp.where(take, refs[0][...].astype(jnp.float32), x)
        power = jnp.sum(x[0] * x[0] + x[1] * x[1], axis=-1, keepdims=True) * (1.0 / W)
        if t:
            r = jnp.where(hi, 3 - j, j)
        else:
            r = jnp.where(hi, lax.rem(8 - u, 8), u)
        o_ref[r] = (x * lax.rsqrt(power + 1e-06)[None]).astype(jnp.bfloat16)


def whiten(spectra, special, hi, t):
    ins = [spectra] + ([special] if t == 0 else [])
    specs = [pl.BlockSpec((2, 4, 1, CH, W), lambda i, hi_ref: (0, i, t, 0, 0))]
    if t == 0:
        specs.append(pl.BlockSpec((2, CH, W), lambda i, hi_ref: (0, 0, 0)))
    if t:
        half = lambda i, hi_ref: (jnp.where(hi_ref[0] == 1, 1 - i, i), 0, 0, 0)
        out_spec = pl.BlockSpec((4, 2, CH, W), half)
    else:
        out_spec = pl.BlockSpec((8, 2, CH, W), lambda i, hi_ref: (0, 0, 0, 0))
    return pl.pallas_call(
        functools.partial(whiten_kernel, t),
        grid_spec=pltpu.PrefetchScalarGridSpec(
            num_scalar_prefetch=1,
            grid=(2,),
            in_specs=specs,
            out_specs=out_spec,
        ),
        out_shape=jax.ShapeDtypeStruct((8, 2, CH, W), jnp.bfloat16),
        compiler_params=pltpu.CompilerParams(vmem_limit_bytes=56 * 1024 * 1024),
        cost_estimate=pl.CostEstimate(flops=2000000, bytes_accessed=1 << 20, transcendentals=0),
        name="whiten",
    )(hi, *ins)


def plane(s, zpos):
    dist = lax.div(s + 1, 2)
    return lax.rem(zpos + 8 + jnp.where(lax.rem(s, 2) == 1, -dist, dist), 8)


def cross_kernel(first, count, z_ref, coef_ref, *refs):
    has_own = first == 0
    own, rest = refs[0:2], refs[2:]
    lows, highs = rest[:count - has_own], rest[count - has_own:2 * (count - has_own)]
    out_ref, left, base, bufs, outs, base_sem, in_sem, out_sem = refs[-8:]

    def load(j, side):
        src = (lows, highs)[side][j]
        return pltpu.make_async_copy(src, bufs.at[j, side], in_sem.at[j, side])

    def load_own(side):
        return pltpu.make_async_copy(own[side], base.at[side], base_sem.at[side])

    for side in range(2):
        load_own(side).start()
    for j in range(count - has_own):
        for side in range(2):
            load(j, side).start()
    for side in range(2):
        load_own(side).wait()
        re = base[side, :, 0].reshape(COLS, W).astype(jnp.float32)
        im = base[side, :, 1].reshape(COLS, W).astype(jnp.float32)
        for o in range(2):
            alpha = coef_ref[o * 4 + side * 2]
            beta = coef_ref[o * 4 + side * 2 + 1]
            rows = pl.ds(o * COLS, COLS)
            left[rows, side * 2 * W:side * 2 * W + W] = (alpha * re + beta * im).astype(jnp.bfloat16)
            left[rows, side * 2 * W + W:side * 2 * W + 2 * W] = (
                alpha * im - beta * re
            ).astype(jnp.bfloat16)

    def store(j):
        g = plane(j + first, z_ref[0])
        return pltpu.make_async_copy(outs.at[j], out_ref.at[g], out_sem.at[j])

    def emit(block, j):
        right = jnp.concatenate(
            [block[side, :, p].reshape(COLS, W) for side in range(2) for p in range(2)], axis=1
        )
        acc = lax.dot_general(
            left[...], right, (((1,), (1,)), ((), ())), preferred_element_type=jnp.float32
        )
        acc = (acc * (1.0 / W)).astype(jnp.bfloat16)
        for o in range(2):
            outs[j, :, o] = acc[o * COLS:(o + 1) * COLS].reshape(NQ, CH, COLS)
        store(j).start()

    if has_own:
        emit(base, 0)

    def body(j, carry):
        for side in range(2):
            pltpu.make_async_copy(own[0], bufs.at[j, side], in_sem.at[j, side]).wait()
        emit(bufs.at[j], j + has_own)
        return carry

    lax.fori_loop(0, count - has_own, body, 0)
    for j in range(count):
        store(j).wait()


def cross(zpos, coef, own, lows, highs, first, prev=None, flops=1 << 30):
    count = len(lows) + (first == 0)
    ins = [*own, *lows, *highs] + ([prev] if prev is not None else [])
    block = (NQ, 2, CH, W)
    return pl.pallas_call(
        functools.partial(cross_kernel, first, count),
        grid_spec=pltpu.PrefetchScalarGridSpec(
            num_scalar_prefetch=2,
            grid=(1,),
            in_specs=[pl.BlockSpec(memory_space=pl.ANY) for b in ins],
            out_specs=pl.BlockSpec(memory_space=pl.ANY),
            scratch_shapes=[
                pltpu.VMEM((2 * COLS, 4 * W), jnp.bfloat16),
                pltpu.VMEM((2, *block), jnp.bfloat16),
                pltpu.VMEM((len(lows), 2, *block), jnp.bfloat16),
                pltpu.VMEM((count, NQ, 2, CH, COLS), jnp.bfloat16),
                pltpu.SemaphoreType.DMA((2,)),
                pltpu.SemaphoreType.DMA((len(lows), 2)),
                pltpu.SemaphoreType.DMA((count,)),
            ],
        ),
        out_shape=jax.ShapeDtypeStruct((NK, NQ, 2, CH, COLS), jnp.bfloat16),
        input_output_aliases={} if prev is None else {len(ins) + 1: 0},
        compiler_params=pltpu.CompilerParams(vmem_limit_bytes=VMEM),
        cost_estimate=pl.CostEstimate(flops=flops, bytes_accessed=4 << 20, transcendentals=0),
        name="cross",
    )(zpos, coef, *ins)


def lags_kernel(t_ref, x1_ref, x0_ref, out_ref):
    x = jnp.concatenate([r[...].reshape(NK * NQ * 2, ROWS, COLS) for r in (x1_ref, x0_ref)])
    x = x.reshape(NK * NQ * 4, ROWS * COLS)
    y = jnp.dot(t_ref[...], x, preferred_element_type=jnp.float32) * math.sqrt(W / NF)
    out_ref[...] = y.reshape(LAGS, ROWS, COLS)


def lags(table, moved):
    n = NK * NQ * 4
    part = pl.BlockSpec((NK * NQ, 2, ROWS, COLS), lambda i: (0, 0, i, 0))
    return pl.pallas_call(
        lags_kernel,
        grid=(CH // ROWS,),
        in_specs=[pl.BlockSpec((LAGS, n), lambda i: (0, 0)), part, part],
        out_specs=pl.BlockSpec((LAGS, ROWS, COLS), lambda i: (0, i, 0)),
        out_shape=jax.ShapeDtypeStruct((LAGS, CH, COLS), jnp.float32),
        compiler_params=pltpu.CompilerParams(vmem_limit_bytes=VMEM),
        cost_estimate=pl.CostEstimate(flops=1 << 29, bytes_accessed=12 << 20, transcendentals=0),
        name="lags",
    )(table, *moved)


def shards(spectra):
    k = lax.axis_index("yh") * X + lax.axis_index("x")
    q = lax.axis_index("yl") * CO + lax.axis_index("co")
    hi = (k > 3).astype(jnp.int32).reshape(1)
    zpos = lax.axis_index("z").astype(jnp.int32).reshape(1)

    special = lax.ppermute(spectra[:, 0], ("yh", "x"), [(1, 0), (2, 1), (3, 2), (0, 3)])
    groups = [[j * NQ + i for j in (g, 7 - g) for i in range(NQ)] for g in range(4)]
    split = spectra.reshape(2, 8, 2, CH, W)

    white = {t: whiten(split, special, hi, t) for t in (1, 0)}

    def regroup(t):
        got = lax.all_to_all(
            white[t],
            PLANE, split_axis=0, concat_axis=0, tiled=True, axis_index_groups=groups,
        )
        return got[:NQ], got[NQ:]

    sin0 = -math.sin(0.0)
    sin64 = -math.sin(math.pi)
    regular = np.array([1, 0, 1, 0, 0, 1, 0, -1], np.float32)
    selfs = np.array([1, sin0, 0, 0, 0, 0, 1, sin64], np.float32)
    is_self = jnp.logical_and(k == 3, q == 0)
    coefs = {0: jnp.where(is_self, selfs, regular), 1: jnp.asarray(regular)}

    up = [(i, (i + 1) % Z) for i in range(Z)]
    dn = [((i + 1) % Z, i) for i in range(Z)]

    def ring(own, before=None, t=0):
        ups, dns = ([], []), ([], [])
        for s in range(4):
            if s == 3:
                near = [(ups[i][n] if d == 0 else dns[i][n]) for i in range(2) for n in range(2) for d in range(2)]
                near_parts = cross(zpos, coefs[t], own, near[:4], near[4:], 0)
                if True:
                    ups, dns = [list(v) for v in ups], [list(v) for v in dns]
                    ups[0][2], dns[1][2], _ = lax.optimization_barrier((ups[0][2], dns[1][2], near_parts))
            if s == 1 and before is not None:
                ups, dns = jax.tree.map(lambda v: lax.optimization_barrier((v, before))[0], (ups, dns))
            for side in range(2):
                if s < 3 or side == 0:
                    ups[side].append(lax.ppermute(ups[side][-1] if s else own[side], "z", up))
                if s < 3 or side == 1:
                    dns[side].append(lax.ppermute(dns[side][-1] if s else own[side], "z", dn))
        return ups, dns, near_parts

    table = jnp.asarray(lag_matrix())
    moved = []
    for t in (1, 0):
        if t == 1:
            own, _ = lax.optimization_barrier((regroup(t), white[0]))
        else:
            own = regroup(t)
            own, _ = lax.optimization_barrier((own, ups[1][2]))
        ups, dns, near_parts = ring(own, parts if t == 0 else None, t)
        parts = near_parts
        far = ([ups[0][2], dns[0][2], ups[0][3]], [ups[1][2], dns[1][2], dns[1][3]])
        parts = cross(zpos, coefs[t], own, *far, 5, parts, FLOPS if t == 0 else 1 << 29)
        parts = parts.reshape(NK * NQ, 2, CH, COLS)
        moved.append(lax.all_to_all(parts, PLANE, split_axis=0, concat_axis=0, tiled=True))
    return lags(table, moved)


def solution(mesh):
    fine = Mesh(mesh.devices.reshape(YH, X, Z, YL, CO), ("yh", "x", "z", "yl", "co"))
    return jax.shard_map(
        shards,
        mesh=fine,
        in_specs=(P(None, ("yh", "x"), ("z", "yl", "co"), None),),
        out_specs=P(None, ("z", "yl", "co"), ("yh", "x")),
        check_vma=False,
    )
```
